32 devices in a mesh: ctx: 16 (over z, x, core), head: 2 (over y).
Axes of the slice: x: 2, y: 2, z: 4, core: 2. Of those that a mesh axis runs over, the one named last changes fastest.
Arguments:
- queries: bfloat16 [4096, 16, 128], P(('ctx', 'head')), may hold values from -8 to 8
- keys: bfloat16 [4096, 16, 128], P(('ctx', 'head')), may hold values from -6 to 6
- values: bfloat16 [4096, 16, 128], P(('ctx', 'head')), may hold values from -6 to 6
- out_grad: bfloat16 [4096, 16, 128], P(('ctx', 'head')), may hold values from -6 to 6
- block_lists: int32 [16, 3], P('ctx'), may hold values from 0 to 15, as said below
Outputs:
- attended: bfloat16 [4096, 16, 128], P(('ctx', 'head'))
- grad_query: bfloat16 [4096, 16, 128], P(('ctx', 'head'))
- grad_key: bfloat16 [4096, 16, 128], P(('ctx', 'head'))
- grad_value: bfloat16 [4096, 16, 128], P(('ctx', 'head'))
The draws below stay inside these ranges and needn't reach their ends.
Inputs may be any that keep to these rules, and one draw needn't show every extreme that they name: `block_lists`: row b begins with b; its other entries are distinct blocks among b - 3 to b - 1, as many of them as exist up to 2, and b again where fewer exist.
All inputs are finite; a program needn't handle non-finite values.
Results may differ from the reference program's by a relative error of at most 0.015.
Values may be sent and summed in bfloat16 or wider, within the bound.
A program may use at most 64 MiB of HBM per device.

```python
import math
import jax
import jax.numpy as jnp
from jax import lax

T_DEV = 256
DH = 128
R = 3
TOPK = 3
NBLK = 16
TOKENS = 4096
HEADS = 16


def draw_queries(key, part):
    result = jnp.clip(jax.random.normal(jax.random.fold_in(key, 1), (TOKENS, HEADS, DH), jnp.float32), -6.0, 6.0)
    return result.astype(jnp.bfloat16)


def draw_keys(key, part):
    result = jnp.clip(jax.random.normal(jax.random.fold_in(key, 2), (TOKENS, HEADS, DH), jnp.float32), -6.0, 6.0)
    return result.astype(jnp.bfloat16)


def draw_block_lists(key, part):
    blocks = jnp.arange(NBLK, dtype=jnp.int32)[:, None]
    offsets = jnp.arange(1, R + 1, dtype=jnp.int32)[None, :]
    candidate_block = blocks - offsets
    noise = jax.random.randint(key, (NBLK, R), 0, 1 << 20, dtype=jnp.int32) * (R + 1) + offsets
    ranking = jnp.where(candidate_block >= 0, noise + (1 << 26), -offsets)
    top_scores, elected_tiles = lax.top_k(ranking, TOPK - 1)
    chosen = jnp.take_along_axis(candidate_block, elected_tiles.astype(jnp.int32), axis=1)
    chosen = jnp.where(chosen >= 0, chosen, blocks)
    return jnp.concatenate([blocks, chosen], axis=1).astype(jnp.int32)


def shard_levels(key, dims, split, least, largest):
    def one(dim, parts):
        steps = jax.random.uniform(jax.random.fold_in(jax.random.fold_in(key, 6), dim), (parts,), jnp.float32, least / len(split), largest / len(split))
        return jnp.repeat(jnp.exp(steps), dims[dim] // parts).reshape((-1,) + (1,) * (len(dims) - dim - 1))

    gain = one(*split[0])
    for cut in split[1:]:
        gain = gain * one(*cut)
    return gain


def scatter_about(rng, dims, width, most, split=(), held_as=jnp.bfloat16):
    factor_of = shard_levels(rng, dims, split, -0.22, 0.18) if split else 1.0
    values = jax.random.normal(rng, dims, jnp.float32) * width * factor_of
    return jnp.minimum(jnp.maximum(values, -most), most).astype(held_as)


def setup_inputs(seed: int = 0) -> dict:
    key_of = jax.random.split(jax.random.key(seed), 6)
    return {
        "queries": draw_queries(jax.random.fold_in(key_of[5], 71), 0),
        "keys": draw_keys(jax.random.fold_in(key_of[5], 71), 0),
        "values": scatter_about(key_of[2], (TOKENS, HEADS, DH), 1.0, 6.0, ((0, 32),)),
        "out_grad": scatter_about(key_of[3], (TOKENS, HEADS, DH), 1.0, 6.0, ((0, 32),)),
        "block_lists": draw_block_lists(jax.random.fold_in(key_of[5], 71), 0),
    }


def reference(queries, keys, values, out_grad, block_lists):
    tokens = queries.shape[0]
    heads_all = queries.shape[1]
    score_scale = 1.0 / math.sqrt(DH)
    key_span = (R + 1) * T_DEV
    padding = jnp.zeros((R * T_DEV, heads_all, DH), queries.dtype)
    key_padded = jnp.concatenate([padding, keys], axis=0)
    value_padded = jnp.concatenate([padding, values], axis=0)
    row_ids = jnp.arange(T_DEV, dtype=jnp.int32)
    lower_tri = row_ids[:, None] >= row_ids[None, :]
    slot_ids = jnp.arange(R + 1, dtype=jnp.int32)
    remote = jnp.repeat(slot_ids < R, T_DEV)

    def step(carried, block_index):
        acc_key, acc_value = carried
        start_row = (block_index * T_DEV).astype(jnp.int32)
        query_block = lax.dynamic_slice_in_dim(queries, start_row, T_DEV, 0).astype(jnp.float32)
        grad_block = lax.dynamic_slice_in_dim(out_grad, start_row, T_DEV, 0).astype(jnp.float32)
        key_block = lax.dynamic_slice_in_dim(key_padded, start_row, key_span, 0).astype(jnp.float32)
        value_block = lax.dynamic_slice_in_dim(value_padded, start_row, key_span, 0).astype(jnp.float32)
        listing = lax.dynamic_index_in_dim(block_lists, block_index, 0, keepdims=False)
        candidate_block = block_index - R + slot_ids
        listed = jnp.any(candidate_block[:, None] == listing[None, :], axis=1) & (candidate_block >= 0)
        allowed = listed[None, :, None] & ((slot_ids[None, :, None] < R) | lower_tri[:, None, :])
        allowed = allowed.reshape(T_DEV, key_span)
        scores = jnp.einsum('thd,shd->hts', query_block, key_block) * score_scale
        scores = jnp.where(allowed[None], scores, -jnp.inf)
        highest = lax.optimization_barrier(jnp.max(scores, axis=2, keepdims=True))
        weights = jnp.exp(scores - highest)
        probability = weights / lax.optimization_barrier(jnp.sum(weights, axis=2, keepdims=True))
        probs_low = lax.optimization_barrier(probability.astype(jnp.bfloat16)).astype(jnp.float32)
        attended = jnp.einsum('hts,shd->thd', probs_low, value_block).astype(jnp.bfloat16)
        grad_probs = jnp.einsum('thd,shd->hts', grad_block, value_block)
        centre = lax.optimization_barrier(jnp.sum(grad_block * attended.astype(jnp.float32), axis=2)).T[:, :, None]
        grad_scores = probability * (grad_probs - centre)
        grad_scores = lax.optimization_barrier(grad_scores.astype(jnp.bfloat16)).astype(jnp.float32)
        grad_query = (jnp.einsum('hts,shd->thd', grad_scores, key_block) * score_scale).astype(jnp.bfloat16)
        part_key = jnp.einsum('hts,thd->shd', grad_scores, query_block) * score_scale
        part_value = jnp.einsum('hts,thd->shd', probs_low, grad_block)
        rounded_key_block = lax.optimization_barrier(part_key.astype(jnp.bfloat16)).astype(jnp.float32)
        lowered_precision_vector = lax.optimization_barrier(part_value.astype(jnp.bfloat16)).astype(jnp.float32)
        part_key = jnp.where(remote[:, None, None], rounded_key_block, part_key)
        part_value = jnp.where(remote[:, None, None], lowered_precision_vector, part_value)
        acc_key = lax.dynamic_update_slice_in_dim(acc_key, lax.dynamic_slice_in_dim(acc_key, start_row, key_span, 0) + part_key, start_row, 0)
        acc_value = lax.dynamic_update_slice_in_dim(acc_value, lax.dynamic_slice_in_dim(acc_value, start_row, key_span, 0) + part_value, start_row, 0)
        return ((acc_key, acc_value), (attended, grad_query))
    zeros = jnp.zeros(((NBLK + R) * T_DEV, heads_all, DH), jnp.float32)
    (acc_key, acc_value), (attended, grad_query) = lax.scan(step, (zeros, zeros), jnp.arange(NBLK, dtype=jnp.int32))
    attended = attended.reshape(tokens, heads_all, DH)
    grad_query = grad_query.reshape(tokens, heads_all, DH)
    grad_key = acc_key[R * T_DEV:].astype(jnp.bfloat16)
    grad_value = acc_value[R * T_DEV:].astype(jnp.bfloat16)
    return (attended, grad_query, grad_key, grad_value)
```

```python
import functools
import math

import jax
import jax.numpy as jnp
from jax import lax
from jax.experimental import pallas as pl
from jax.experimental.pallas import tpu as pltpu
from jax.sharding import PartitionSpec as P

R = 3
MESH = pl.DeviceIdType.MESH
BF16, F32 = jnp.bfloat16, jnp.float32


def dot(a, b, ca, cb):
    return lax.dot_general(a, b, (((ca,), (cb,)), ((), ())), preferred_element_type=F32)


def kernel(
    nctx, nhead, chunks, lists_ref, x_ref, out_ref,
    blk, near, mid, far, p1, p2, p3, bud, ra, rb, own, outb,
    s_loc, s_yin, r_yin, s_ctx, r_ctx, s_gr, r_gr, s_out, r_out, s_oloc,
):
    ctx = lax.axis_index("ctx")
    head = lax.axis_index("head")
    heads = blk.shape[2]
    length = blk.shape[3]
    width = blk.shape[4]
    rows = length // nhead
    held = heads * chunks
    even = lax.rem(ctx, 2) == 0
    odd = lax.rem(ctx, 2) == 1
    buddy = ctx + 1 - 2 * lax.rem(ctx, 2)
    score_scale = 1.0 / math.sqrt(width)
    mine = pl.ds(pl.multiple_of(head * rows, rows), rows)

    def mate(step):
        return lax.rem(head + step, nhead)

    barrier = pltpu.get_barrier_semaphore()
    for step in range(1, nhead):
        pl.semaphore_signal(barrier, inc=1, device_id=(ctx, mate(step)), device_id_type=MESH)
    near_by = 0
    for away in (-3, -1, 1, 3):
        other = ctx + away
        inside = (other >= 0) & (other < nctx)

        @pl.when(inside)
        def _():
            pl.semaphore_signal(barrier, inc=1, device_id=(other, head), device_id_type=MESH)

        near_by = near_by + inside.astype(jnp.int32)
    pl.semaphore_wait(barrier, near_by + (nhead - 1))

    def yin_out(j, kind, step):
        to = mate(step)
        return pltpu.make_async_remote_copy(
            src_ref=x_ref.at[pl.ds(2 * kind, 2), pl.ds(to * held + j * heads, heads)],
            dst_ref=blk.at[j, pl.ds(2 * kind, 2), :, mine],
            send_sem=s_yin.at[j, kind, step - 1],
            recv_sem=r_yin.at[j, kind, step - 1],
            device_id=(ctx, to),
            device_id_type=MESH,
        )

    def yin_in(j, kind, step):
        source = lax.rem(head + nhead - step, nhead)
        theirs = pl.ds(pl.multiple_of(source * rows, rows), rows)
        return pltpu.make_async_remote_copy(
            src_ref=x_ref.at[pl.ds(2 * kind, 2), pl.ds(j * heads, heads)],
            dst_ref=blk.at[j, pl.ds(2 * kind, 2), :, theirs],
            send_sem=s_yin.at[j, kind, step - 1],
            recv_sem=r_yin.at[j, kind, step - 1],
            device_id=(ctx, source),
            device_id_type=MESH,
        )

    def yin_local(j, kind):
        return pltpu.make_async_copy(
            x_ref.at[pl.ds(2 * kind, 2), pl.ds(head * held + j * heads, heads)],
            blk.at[j, pl.ds(2 * kind, 2), :, mine],
            s_loc.at[j, kind],
        )

    def yin_start(j, kind):
        for step in range(1, nhead):
            yin_out(j, kind, step).start()
        yin_local(j, kind).start()

    def yin_wait(j, kind):
        for step in range(1, nhead):
            yin_in(j, kind, step).wait_recv()
        yin_local(j, kind).wait()

    def ctx_copy(src, dst, sems, recvs, j, which, to):
        return pltpu.make_async_remote_copy(
            src_ref=src,
            dst_ref=dst,
            send_sem=sems.at[j, which],
            recv_sem=recvs.at[j, which],
            device_id=(to, head),
            device_id_type=MESH,
        )

    def kv(j):
        return blk.at[j, pl.ds(0, 2)]

    def send_near(j):
        return ctx_copy(kv(j), near.at[j], s_ctx, r_ctx, j, 0, ctx + 1)

    def send_far(j):
        return ctx_copy(kv(j), far.at[j], s_ctx, r_ctx, j, 1, ctx + 3)

    def pass_near(j):
        return ctx_copy(near.at[j], mid.at[j], s_ctx, r_ctx, j, 2, buddy)

    def pass_far(j):
        return ctx_copy(far.at[j], mid.at[j], s_ctx, r_ctx, j, 2, buddy)

    def give_mid(j):
        return ctx_copy(p2.at[j], bud.at[j], s_gr, r_gr, j, 0, buddy)

    def give_near(j):
        return ctx_copy(p1.at[j], ra.at[j], s_gr, r_gr, j, 1, ctx - 1)

    def give_far(j):
        return ctx_copy(p3.at[j], rb.at[j], s_gr, r_gr, j, 2, ctx - 3)

    has1, has3 = ctx >= 1, ctx >= 3
    to1, to3 = ctx + 1 < nctx, ctx + 3 < nctx
    pass1 = even & has1
    pass3 = odd & has3
    mid_in = ctx >= 2
    bud_in = (even & has1) | (odd & has3)

    def yout_out(j, kind, step):
        to = mate(step)
        part = pl.ds(pl.multiple_of(to * rows, rows), rows)
        return pltpu.make_async_remote_copy(
            src_ref=outb.at[j, pl.ds(2 * kind, 2), :, part],
            dst_ref=out_ref.at[pl.ds(2 * kind, 2), pl.ds(head * held + j * heads, heads)],
            send_sem=s_out.at[j, kind, step - 1],
            recv_sem=r_out.at[j, kind, step - 1],
            device_id=(ctx, to),
            device_id_type=MESH,
        )

    def yout_in(j, kind, step):
        source = lax.rem(head + nhead - step, nhead)
        return pltpu.make_async_remote_copy(
            src_ref=outb.at[j, pl.ds(2 * kind, 2), :, mine],
            dst_ref=out_ref.at[pl.ds(2 * kind, 2), pl.ds(source * held + j * heads, heads)],
            send_sem=s_out.at[j, kind, step - 1],
            recv_sem=r_out.at[j, kind, step - 1],
            device_id=(ctx, source),
            device_id_type=MESH,
        )

    def yout_local(j, kind):
        return pltpu.make_async_copy(
            outb.at[j, pl.ds(2 * kind, 2), :, mine],
            out_ref.at[pl.ds(2 * kind, 2), pl.ds(head * held + j * heads, heads)],
            s_oloc.at[j, kind],
        )

    def yout_start(j, kind):
        for step in range(1, nhead):
            yout_out(j, kind, step).start()
        yout_local(j, kind).start()

    addend = []
    for distance in range(1, R + 1):
        block = ctx - distance
        listed = block == lists_ref[0, 0]
        for entry in range(1, lists_ref.shape[1]):
            listed = listed | (block == lists_ref[0, entry])
        addend.append(jnp.where(listed & (block >= 0), jnp.float32(0), jnp.float32(-jnp.inf)))

    def attend(j, h):
        key0, value0 = blk[j, 0, h], blk[j, 1, h]
        query, grad = blk[j, 2, h], blk[j, 3, h]
        windows = (near, mid, far)
        keys = [key0] + [w[j, 0, h] for w in windows]
        values = [value0] + [w[j, 1, h] for w in windows]
        scores = [dot(k, query, 1, 1) for k in keys]
        s_ids = lax.broadcasted_iota(jnp.int32, (length, length), 0)
        t_ids = lax.broadcasted_iota(jnp.int32, (length, length), 1)
        scores[0] = jnp.where(s_ids <= t_ids, scores[0], -jnp.inf)
        for d in range(1, R + 1):
            scores[d] = scores[d] + addend[d - 1]
        highest = functools.reduce(
            jnp.maximum, [jnp.max(s, axis=0, keepdims=True) for s in scores]
        )
        to_exp2 = score_scale * math.log2(math.e)
        weights = [jnp.exp2((s - highest) * to_exp2) for s in scores]
        total = functools.reduce(
            jnp.add, [jnp.sum(w, axis=0, keepdims=True) for w in weights]
        )
        inverse = 1.0 / total
        probs = [w * inverse for w in weights]
        low = [p.astype(BF16) for p in probs]
        attended = functools.reduce(
            jnp.add, [dot(p, v, 0, 0) for p, v in zip(low, values)]
        ).astype(BF16)
        outb[j, 0, h] = attended
        product = grad.astype(F32) * attended.astype(F32)
        centre = jnp.sum(product.T, axis=0, keepdims=True)
        slopes = [
            (p * (dot(v, grad, 1, 1) - centre)).astype(BF16) for p, v in zip(probs, values)
        ]
        grad_query = functools.reduce(
            jnp.add, [dot(g, k, 0, 0) for g, k in zip(slopes, keys)]
        )
        outb[j, 1, h] = (grad_query * score_scale).astype(BF16)
        for d, slot in enumerate((own, p1, p2, p3)):
            slot[j, 0, h] = (dot(slopes[d], query, 1, 0) * score_scale).astype(slot.dtype)
            slot[j, 1, h] = dot(low[d], grad, 1, 0).astype(slot.dtype)

    order = [(0, 0)]
    for j in range(chunks):
        if j + 1 < chunks:
            order.append((j + 1, 0))
        order.append((j, 1))
    for j, kind in order:
        yin_start(j, kind)
    for distance, slot in ((1, near), (2, mid), (3, far)):

        @pl.when(ctx < distance)
        def _():
            slot[...] = jnp.zeros_like(slot)

    def stage(t, lag, run):
        @pl.when((t >= lag) & (t < lag + chunks))
        def _():
            run(t - lag)

    def forward(j):
        yin_wait(j, 0)
        pl.when(to3)(lambda: send_far(j).start())
        pl.when(to1)(lambda: send_near(j).start())

    def relay(j):
        pl.when(has3)(lambda: send_far(j).wait_recv())
        pl.when(pass3)(lambda: pass_far(j).start())
        pl.when(has1)(lambda: send_near(j).wait_recv())
        pl.when(pass1)(lambda: pass_near(j).start())

    def compute(j):
        yin_wait(j, 1)
        pl.when(mid_in)(lambda: pass_near(j).wait_recv())

        def one(h, carry):
            attend(j, h)
            return carry

        lax.fori_loop(0, heads, one, 0)
        pl.when(mid_in)(lambda: give_mid(j).start())
        pl.when(even & has3)(lambda: give_far(j).start())
        pl.when(odd)(lambda: give_near(j).start())
        yout_start(j, 0)

    def combine(j):
        pl.when(bud_in)(lambda: give_mid(j).wait_recv())

        @pl.when(pass1)
        def _():
            p1[j] = (p1[j].astype(F32) + bud[j].astype(F32)).astype(BF16)
            give_near(j).start()

        @pl.when(pass3)
        def _():
            p3[j] = (p3[j].astype(F32) + bud[j].astype(F32)).astype(BF16)
            give_far(j).start()

    def finish(j):
        @pl.when(to1)
        def _():
            give_near(j).wait_recv()
            own[j] = own[j] + ra[j].astype(F32)

        @pl.when(to3)
        def _():
            give_far(j).wait_recv()
            own[j] = own[j] + rb[j].astype(F32)

        outb[j, pl.ds(2, 2)] = own[j].astype(BF16)
        yout_start(j, 1)

    def body(t, carry):
        stage(t, 0, forward)
        stage(t, 1, relay)
        stage(t, 2, compute)
        stage(t, 3, combine)
        stage(t, 4, finish)
        return carry

    lax.fori_loop(0, chunks + 4, body, 0)

    def drain(j, carry):
        for kind in range(2):
            for step in range(1, nhead):
                yin_out(j, kind, step).wait_send()
                yout_out(j, kind, step).wait_send()
                yout_in(j, kind, step).wait_recv()
            yout_local(j, kind).wait()
        pl.when(to1)(lambda: send_near(j).wait_send())
        pl.when(to3)(lambda: send_far(j).wait_send())
        pl.when(pass1)(lambda: pass_near(j).wait_send())
        pl.when(pass3)(lambda: pass_far(j).wait_send())
        pl.when(mid_in)(lambda: give_mid(j).wait_send())
        pl.when(has1)(lambda: give_near(j).wait_send())
        pl.when(has3)(lambda: give_far(j).wait_send())
        return carry

    lax.fori_loop(0, chunks, drain, 0)


def local(nctx, nhead, queries, keys, values, out_grad, block_lists):
    rows, heads_all, width = queries.shape
    length = rows * nhead
    held = heads_all // nhead
    chunks = 4
    heads = held // chunks
    stacked = jnp.stack([a.transpose(1, 0, 2) for a in (keys, values, queries, out_grad)])
    half = pltpu.VMEM((chunks, 2, heads, length, width), BF16)
    dma = pltpu.SemaphoreType.DMA
    flops = 6 * 2 * held * length * length * (R + 1) * width
    out = pl.pallas_call(
        functools.partial(kernel, nctx, nhead, chunks),
        out_shape=jax.ShapeDtypeStruct((4, heads_all, rows, width), BF16),
        in_specs=[
            pl.BlockSpec(memory_space=pltpu.SMEM),
            pl.BlockSpec(memory_space=pl.ANY),
        ],
        out_specs=pl.BlockSpec(memory_space=pl.ANY),
        scratch_shapes=[
            pltpu.VMEM((chunks, 4, heads, length, width), BF16),
            half, half, half,
            half, half, half,
            half, half, half,
            pltpu.VMEM((chunks, 2, heads, length, width), F32),
            pltpu.VMEM((chunks, 4, heads, length, width), BF16),
            dma((chunks, 2)),
            dma((chunks, 2, nhead - 1)),
            dma((chunks, 2, nhead - 1)),
            dma((chunks, 3)),
            dma((chunks, 3)),
            dma((chunks, 3)),
            dma((chunks, 3)),
            dma((chunks, 2, nhead - 1)),
            dma((chunks, 2, nhead - 1)),
            dma((chunks, 2)),
        ],
        compiler_params=pltpu.CompilerParams(
            collective_id=0, has_side_effects=True, vmem_limit_bytes=48 * 1024 * 1024
        ),
        cost_estimate=pl.CostEstimate(
            flops=flops, bytes_accessed=16 * rows * heads_all * width, transcendentals=0
        ),
    )(block_lists, stacked)
    return tuple(out[a].transpose(1, 0, 2) for a in range(4))


def solution(mesh):
    split = P(("ctx", "head"), None, None)
    return jax.shard_map(
        functools.partial(local, mesh.shape["ctx"], mesh.shape["head"]),
        mesh=mesh,
        in_specs=(split, split, split, split, P("ctx", None)),
        out_specs=(split, split, split, split),
        check_vma=False,
    )
```

```python
import functools
import math

import jax
import jax.numpy as jnp
from jax import lax
from jax.experimental import pallas as pl
from jax.experimental.pallas import tpu as pltpu
from jax.sharding import PartitionSpec as P

R = 3
MESH = pl.DeviceIdType.MESH
BF16, F32 = jnp.bfloat16, jnp.float32


def dot(a, b, ca, cb):
    return lax.dot_general(a, b, (((ca,), (cb,)), ((), ())), preferred_element_type=F32)


def kernel(
    nctx, nhead, chunks, lists_ref, x_ref, out_ref,
    blk, near, mid, far, p1, p2, p3, bud, hop, ra, rb, own, outb,
    s_loc, s_yin, r_yin, s_ctx, r_ctx, s_gr, r_gr, s_out, r_out, s_oloc,
):
    ctx = lax.axis_index("ctx")
    head = lax.axis_index("head")
    heads = blk.shape[2]
    length = blk.shape[3]
    width = blk.shape[4]
    rows = length // nhead
    held = heads * chunks
    even = lax.rem(ctx, 2) == 0
    odd = lax.rem(ctx, 2) == 1
    place = lax.rem(ctx, 4)
    buddy = ctx + 1 - 2 * lax.rem(ctx, 2)
    score_scale = 1.0 / math.sqrt(width)
    mine = pl.ds(pl.multiple_of(head * rows, rows), rows)

    def mate(step):
        return lax.rem(head + step, nhead)

    barrier = pltpu.get_barrier_semaphore()
    for step in range(1, nhead):
        pl.semaphore_signal(barrier, inc=1, device_id=(ctx, mate(step)), device_id_type=MESH)
    near_by = 0
    for away in (-3, -1, 1, 3):
        other = ctx + away
        inside = (other >= 0) & (other < nctx)

        @pl.when(inside)
        def _():
            pl.semaphore_signal(barrier, inc=1, device_id=(other, head), device_id_type=MESH)

        near_by = near_by + inside.astype(jnp.int32)
    first, third, last = place == 0, place == 2, place == 3
    has1, has3 = ctx >= 1, ctx >= 3
    for role, other in ((third & has3, ctx - 2), (first & has1, ctx + 2)):

        @pl.when(role)
        def _():
            pl.semaphore_signal(barrier, inc=1, device_id=(other, head), device_id_type=MESH)

        near_by = near_by + role.astype(jnp.int32)
    pl.semaphore_wait(barrier, near_by + (nhead - 1))

    def yin_out(j, kind, step):
        to = mate(step)
        return pltpu.make_async_remote_copy(
            src_ref=x_ref.at[pl.ds(2 * kind, 2), pl.ds(to * held + j * heads, heads)],
            dst_ref=blk.at[j, pl.ds(2 * kind, 2), :, mine],
            send_sem=s_yin.at[j, kind, step - 1],
            recv_sem=r_yin.at[j, kind, step - 1],
            device_id=(ctx, to),
            device_id_type=MESH,
        )

    def yin_in(j, kind, step):
        source = lax.rem(head + nhead - step, nhead)
        theirs = pl.ds(pl.multiple_of(source * rows, rows), rows)
        return pltpu.make_async_remote_copy(
            src_ref=x_ref.at[pl.ds(2 * kind, 2), pl.ds(j * heads, heads)],
            dst_ref=blk.at[j, pl.ds(2 * kind, 2), :, theirs],
            send_sem=s_yin.at[j, kind, step - 1],
            recv_sem=r_yin.at[j, kind, step - 1],
            device_id=(ctx, source),
            device_id_type=MESH,
        )

    def yin_local(j, kind):
        return pltpu.make_async_copy(
            x_ref.at[pl.ds(2 * kind, 2), pl.ds(head * held + j * heads, heads)],
            blk.at[j, pl.ds(2 * kind, 2), :, mine],
            s_loc.at[j, kind],
        )

    def yin_start(j, kind):
        for step in range(1, nhead):
            yin_out(j, kind, step).start()
        yin_local(j, kind).start()

    def yin_wait(j, kind):
        for step in range(1, nhead):
            yin_in(j, kind, step).wait_recv()
        yin_local(j, kind).wait()

    def ctx_copy(src, dst, sems, recvs, j, which, to, lands=None):
        return pltpu.make_async_remote_copy(
            src_ref=src,
            dst_ref=dst,
            send_sem=sems.at[j, which],
            recv_sem=recvs.at[j, which if lands is None else lands],
            device_id=(to, head),
            device_id_type=MESH,
        )

    def kv(j):
        return blk.at[j, pl.ds(0, 2)]

    def send_near(j):
        return ctx_copy(kv(j), near.at[j], s_ctx, r_ctx, j, 0, ctx + 1)

    def send_far(j):
        return ctx_copy(kv(j), far.at[j], s_ctx, r_ctx, j, 1, ctx + 3)

    def pass_near(j):
        return ctx_copy(near.at[j], mid.at[j], s_ctx, r_ctx, j, 2, buddy)

    def pass_far(j):
        return ctx_copy(far.at[j], mid.at[j], s_ctx, r_ctx, j, 2, buddy)

    def hop_near(j):
        return ctx_copy(far.at[j], near.at[j], s_ctx, r_ctx, j, 3, ctx - 2, 0)

    def hop_back(j):
        return ctx_copy(p1.at[j], hop.at[j], s_gr, r_gr, j, 3, ctx + 2)

    def give_mid(j):
        return ctx_copy(p2.at[j], bud.at[j], s_gr, r_gr, j, 0, buddy)

    def give_near(j):
        return ctx_copy(p1.at[j], ra.at[j], s_gr, r_gr, j, 1, ctx - 1)

    def give_far(j):
        return ctx_copy(p3.at[j], rb.at[j], s_gr, r_gr, j, 2, ctx - 3)

    to1, to3 = (ctx + 1 < nctx) & ~last, ctx + 3 < nctx
    hop1, hop3 = first & has1, third & has3
    pass1 = even & has1
    pass3 = odd & has3
    mid_in = ctx >= 2
    bud_in = (even & has1) | (odd & has3)

    def yout_out(j, kind, step):
        to = mate(step)
        part = pl.ds(pl.multiple_of(to * rows, rows), rows)
        return pltpu.make_async_remote_copy(
            src_ref=outb.at[j, pl.ds(2 * kind, 2), :, part],
            dst_ref=out_ref.at[pl.ds(2 * kind, 2), pl.ds(head * held + j * heads, heads)],
            send_sem=s_out.at[j, kind, step - 1],
            recv_sem=r_out.at[j, kind, step - 1],
            device_id=(ctx, to),
            device_id_type=MESH,
        )

    def yout_in(j, kind, step):
        source = lax.rem(head + nhead - step, nhead)
        return pltpu.make_async_remote_copy(
            src_ref=outb.at[j, pl.ds(2 * kind, 2), :, mine],
            dst_ref=out_ref.at[pl.ds(2 * kind, 2), pl.ds(source * held + j * heads, heads)],
            send_sem=s_out.at[j, kind, step - 1],
            recv_sem=r_out.at[j, kind, step - 1],
            device_id=(ctx, source),
            device_id_type=MESH,
        )

    def yout_local(j, kind):
        return pltpu.make_async_copy(
            outb.at[j, pl.ds(2 * kind, 2), :, mine],
            out_ref.at[pl.ds(2 * kind, 2), pl.ds(head * held + j * heads, heads)],
            s_oloc.at[j, kind],
        )

    def yout_start(j, kind):
        for step in range(1, nhead):
            yout_out(j, kind, step).start()
        yout_local(j, kind).start()

    addend = []
    for distance in range(1, R + 1):
        block = ctx - distance
        listed = block == lists_ref[0, 0]
        for entry in range(1, lists_ref.shape[1]):
            listed = listed | (block == lists_ref[0, entry])
        addend.append(jnp.where(listed & (block >= 0), jnp.float32(0), jnp.float32(-jnp.inf)))

    def attend(j, h):
        key0, value0 = blk[j, 0, h], blk[j, 1, h]
        query, grad = blk[j, 2, h], blk[j, 3, h]
        windows = (near, mid, far)
        keys = [key0] + [w[j, 0, h] for w in windows]
        values = [value0] + [w[j, 1, h] for w in windows]
        scores = [dot(k, query, 1, 1) for k in keys]
        s_ids = lax.broadcasted_iota(jnp.int32, (length, length), 0)
        t_ids = lax.broadcasted_iota(jnp.int32, (length, length), 1)
        scores[0] = jnp.where(s_ids <= t_ids, scores[0], -jnp.inf)
        for d in range(1, R + 1):
            scores[d] = scores[d] + addend[d - 1]
        highest = functools.reduce(
            jnp.maximum, [jnp.max(s, axis=0, keepdims=True) for s in scores]
        )
        to_exp2 = score_scale * math.log2(math.e)
        weights = [jnp.exp2((s - highest) * to_exp2) for s in scores]
        total = functools.reduce(
            jnp.add, [jnp.sum(w, axis=0, keepdims=True) for w in weights]
        )
        inverse = 1.0 / total
        probs = [w * inverse for w in weights]
        low = [p.astype(BF16) for p in probs]
        attended = functools.reduce(
            jnp.add, [dot(p, v, 0, 0) for p, v in zip(low, values)]
        ).astype(BF16)
        outb[j, 0, h] = attended
        product = grad.astype(F32) * attended.astype(F32)
        centre = jnp.sum(product.T, axis=0, keepdims=True)
        slopes = [
            (p * (dot(v, grad, 1, 1) - centre)).astype(BF16) for p, v in zip(probs, values)
        ]
        grad_query = functools.reduce(
            jnp.add, [dot(g, k, 0, 0) for g, k in zip(slopes, keys)]
        )
        outb[j, 1, h] = (grad_query * score_scale).astype(BF16)
        for d, slot in enumerate((own, p1, p2, p3)):
            slot[j, 0, h] = (dot(slopes[d], query, 1, 0) * score_scale).astype(slot.dtype)
            slot[j, 1, h] = dot(low[d], grad, 1, 0).astype(slot.dtype)

    order = [(0, 0)]
    for j in range(chunks):
        if j + 1 < chunks:
            order.append((j + 1, 0))
        order.append((j, 1))
    for j, kind in order:
        yin_start(j, kind)
    for distance, slot in ((1, near), (2, mid), (3, far)):

        @pl.when(ctx < distance)
        def _():
            slot[...] = jnp.zeros_like(slot)

    def stage(t, lag, run):
        @pl.when((t >= lag) & (t < lag + chunks))
        def _():
            run(t - lag)

    def forward(j):
        yin_wait(j, 0)
        pl.when(to3)(lambda: send_far(j).start())
        pl.when(to1)(lambda: send_near(j).start())

    def relay(j):
        pl.when(has3)(lambda: send_far(j).wait_recv())
        pl.when(hop3)(lambda: hop_near(j).start())
        pl.when(pass3)(lambda: pass_far(j).start())
        pl.when(has1 & ~first)(lambda: send_near(j).wait_recv())
        pl.when(third)(lambda: pass_near(j).start())

    def relay_again(j):
        @pl.when(hop1)
        def _():
            send_near(j).wait_recv()
            pass_near(j).start()

    def compute(j):
        yin_wait(j, 1)
        pl.when(mid_in)(lambda: pass_near(j).wait_recv())

        def one(h, carry):
            attend(j, h)
            return carry

        lax.fori_loop(0, heads, one, 0)
        pl.when(mid_in)(lambda: give_mid(j).start())
        pl.when(hop1)(lambda: give_far(j).start())
        pl.when(odd)(lambda: give_near(j).start())
        yout_start(j, 0)

    def combine(j):
        pl.when(bud_in)(lambda: give_mid(j).wait_recv())

        @pl.when(pass1)
        def _():
            p1[j] = (p1[j].astype(F32) + bud[j].astype(F32)).astype(BF16)
            pl.when(third)(lambda: give_near(j).start())
            pl.when(first)(lambda: hop_back(j).start())

        @pl.when(pass3)
        def _():
            p3[j] = (p3[j].astype(F32) + bud[j].astype(F32)).astype(BF16)
            give_far(j).start()

    def combine_again(j):
        @pl.when(hop3)
        def _():
            hop_back(j).wait_recv()
            p3[j] = (p3[j].astype(F32) + hop[j].astype(F32)).astype(BF16)
            give_far(j).start()

    def finish(j):
        @pl.when(to1)
        def _():
            give_near(j).wait_recv()
            own[j] = own[j] + ra[j].astype(F32)

        @pl.when(to3)
        def _():
            give_far(j).wait_recv()
            own[j] = own[j] + rb[j].astype(F32)

        outb[j, pl.ds(2, 2)] = own[j].astype(BF16)
        yout_start(j, 1)

    def body(t, carry):
        stage(t, 0, forward)
        stage(t, 1, relay)
        stage(t, 3, relay_again)
        stage(t, 4, compute)
        stage(t, 5, combine)
        stage(t, 6, combine_again)
        stage(t, 8, finish)
        return carry

    lax.fori_loop(0, chunks + 8, body, 0)

    def drain(j, carry):
        for kind in range(2):
            for step in range(1, nhead):
                yin_out(j, kind, step).wait_send()
                yout_out(j, kind, step).wait_send()
                yout_in(j, kind, step).wait_recv()
            yout_local(j, kind).wait()
        pl.when(to1)(lambda: send_near(j).wait_send())
        pl.when(to3)(lambda: send_far(j).wait_send())
        pl.when(pass1)(lambda: pass_near(j).wait_send())
        pl.when(pass3)(lambda: pass_far(j).wait_send())
        pl.when(mid_in)(lambda: give_mid(j).wait_send())
        pl.when(hop3)(lambda: hop_near(j).wait_send())
        pl.when(hop1)(lambda: hop_back(j).wait_send())
        pl.when(has1 & ~first)(lambda: give_near(j).wait_send())
        pl.when(has3)(lambda: give_far(j).wait_send())
        return carry

    lax.fori_loop(0, chunks, drain, 0)


def local(nctx, nhead, queries, keys, values, out_grad, block_lists):
    rows, heads_all, width = queries.shape
    length = rows * nhead
    held = heads_all // nhead
    chunks = 8
    heads = held // chunks
    stacked = jnp.stack([a.transpose(1, 0, 2) for a in (keys, values, queries, out_grad)])
    half = pltpu.VMEM((chunks, 2, heads, length, width), BF16)
    dma = pltpu.SemaphoreType.DMA
    flops = 6 * 2 * held * length * length * (R + 1) * width
    out = pl.pallas_call(
        functools.partial(kernel, nctx, nhead, chunks),
        out_shape=jax.ShapeDtypeStruct((4, heads_all, rows, width), BF16),
        in_specs=[
            pl.BlockSpec(memory_space=pltpu.SMEM),
            pl.BlockSpec(memory_space=pl.ANY),
        ],
        out_specs=pl.BlockSpec(memory_space=pl.ANY),
        scratch_shapes=[
            pltpu.VMEM((chunks, 4, heads, length, width), BF16),
            half, half, half,
            half, half, half,
            half, half, half, half,
            pltpu.VMEM((chunks, 2, heads, length, width), F32),
            pltpu.VMEM((chunks, 4, heads, length, width), BF16),
            dma((chunks, 2)),
            dma((chunks, 2, nhead - 1)),
            dma((chunks, 2, nhead - 1)),
            dma((chunks, 4)),
            dma((chunks, 3)),
            dma((chunks, 4)),
            dma((chunks, 4)),
            dma((chunks, 2, nhead - 1)),
            dma((chunks, 2, nhead - 1)),
            dma((chunks, 2)),
        ],
        compiler_params=pltpu.CompilerParams(
            collective_id=0, has_side_effects=True, vmem_limit_bytes=48 * 1024 * 1024
        ),
        cost_estimate=pl.CostEstimate(
            flops=flops, bytes_accessed=16 * rows * heads_all * width, transcendentals=0
        ),
    )(block_lists, stacked)
    return tuple(out[a].transpose(1, 0, 2) for a in range(4))


def solution(mesh):
    split = P(("ctx", "head"), None, None)
    return jax.shard_map(
        functools.partial(local, mesh.shape["ctx"], mesh.shape["head"]),
        mesh=mesh,
        in_specs=(split, split, split, split, P("ctx", None)),
        out_specs=(split, split, split, split),
        check_vma=False,
    )
```

```python
import functools
import math

import jax
import jax.numpy as jnp
from jax import lax
from jax.experimental import pallas as pl
from jax.experimental.pallas import tpu as pltpu
from jax.sharding import PartitionSpec as P

R = 3
MESH = pl.DeviceIdType.MESH
BF16, F32 = jnp.bfloat16, jnp.float32


def dot(a, b, ca, cb):
    return lax.dot_general(a, b, (((ca,), (cb,)), ((), ())), preferred_element_type=F32)


def kernel(
    nctx, nhead, chunks, lists_ref, x_ref, out0, out1, out2, out3,
    out_ref, blk, near, mid, far, p1, p2, p3, bud, hop, ra, rb, own, outb,
    s_loc, s_yin, r_yin, s_ctx, r_ctx, s_gr, r_gr, s_out, r_out, s_oloc,
):
    ctx = lax.axis_index("ctx")
    head = lax.axis_index("head")
    heads = blk.shape[2]
    length = blk.shape[3]
    width = blk.shape[4]
    rows = length // nhead
    held = heads * chunks
    even = lax.rem(ctx, 2) == 0
    odd = lax.rem(ctx, 2) == 1
    place = lax.rem(ctx, 4)
    buddy = ctx + 1 - 2 * lax.rem(ctx, 2)
    score_scale = 1.0 / math.sqrt(width)
    mine = pl.ds(pl.multiple_of(head * rows, rows), rows)

    def mate(step):
        return lax.rem(head + step, nhead)

    barrier = pltpu.get_barrier_semaphore()
    for step in range(1, nhead):
        pl.semaphore_signal(barrier, inc=1, device_id=(ctx, mate(step)), device_id_type=MESH)
    near_by = 0
    for away in (-3, -1, 1, 3):
        other = ctx + away
        inside = (other >= 0) & (other < nctx)

        @pl.when(inside)
        def _():
            pl.semaphore_signal(barrier, inc=1, device_id=(other, head), device_id_type=MESH)

        near_by = near_by + inside.astype(jnp.int32)
    first, third, last = place == 0, place == 2, place == 3
    has1, has3 = ctx >= 1, ctx >= 3
    for role, other in ((third & has3, ctx - 2), (first & has1, ctx + 2)):

        @pl.when(role)
        def _():
            pl.semaphore_signal(barrier, inc=1, device_id=(other, head), device_id_type=MESH)

        near_by = near_by + role.astype(jnp.int32)
    pl.semaphore_wait(barrier, near_by + (nhead - 1))

    def yin_out(j, kind, step):
        to = mate(step)
        return pltpu.make_async_remote_copy(
            src_ref=x_ref.at[pl.ds(2 * kind, 2), pl.ds(to * held + j * heads, heads)],
            dst_ref=blk.at[j, pl.ds(2 * kind, 2), :, mine],
            send_sem=s_yin.at[j, kind, step - 1],
            recv_sem=r_yin.at[j, kind, step - 1],
            device_id=(ctx, to),
            device_id_type=MESH,
        )

    def yin_in(j, kind, step):
        source = lax.rem(head + nhead - step, nhead)
        theirs = pl.ds(pl.multiple_of(source * rows, rows), rows)
        return pltpu.make_async_remote_copy(
            src_ref=x_ref.at[pl.ds(2 * kind, 2), pl.ds(j * heads, heads)],
            dst_ref=blk.at[j, pl.ds(2 * kind, 2), :, theirs],
            send_sem=s_yin.at[j, kind, step - 1],
            recv_sem=r_yin.at[j, kind, step - 1],
            device_id=(ctx, source),
            device_id_type=MESH,
        )

    def yin_local(j, kind):
        return pltpu.make_async_copy(
            x_ref.at[pl.ds(2 * kind, 2), pl.ds(head * held + j * heads, heads)],
            blk.at[j, pl.ds(2 * kind, 2), :, mine],
            s_loc.at[j, kind],
        )

    def yin_start(j, kind):
        for step in range(1, nhead):
            yin_out(j, kind, step).start()
        yin_local(j, kind).start()

    def yin_wait(j, kind):
        for step in range(1, nhead):
            yin_in(j, kind, step).wait_recv()
        yin_local(j, kind).wait()

    def ctx_copy(src, dst, sems, recvs, j, which, to, lands=None):
        return pltpu.make_async_remote_copy(
            src_ref=src,
            dst_ref=dst,
            send_sem=sems.at[j, which],
            recv_sem=recvs.at[j, which if lands is None else lands],
            device_id=(to, head),
            device_id_type=MESH,
        )

    def kv(j):
        return blk.at[j, pl.ds(0, 2)]

    def send_near(j):
        return ctx_copy(kv(j), near.at[j], s_ctx, r_ctx, j, 0, ctx + 1)

    def send_far(j):
        return ctx_copy(kv(j), far.at[j], s_ctx, r_ctx, j, 1, ctx + 3)

    def pass_near(j):
        return ctx_copy(near.at[j], mid.at[j], s_ctx, r_ctx, j, 2, buddy)

    def pass_far(j):
        return ctx_copy(far.at[j], mid.at[j], s_ctx, r_ctx, j, 2, buddy)

    def hop_near(j):
        return ctx_copy(far.at[j], near.at[j], s_ctx, r_ctx, j, 3, ctx - 2, 0)

    def hop_back(j):
        return ctx_copy(p1.at[j], hop.at[j], s_gr, r_gr, j, 3, ctx + 2)

    def give_mid(j):
        return ctx_copy(p2.at[j], bud.at[j], s_gr, r_gr, j, 0, buddy)

    def give_near(j):
        return ctx_copy(p1.at[j], ra.at[j], s_gr, r_gr, j, 1, ctx - 1)

    def give_far(j):
        return ctx_copy(p3.at[j], rb.at[j], s_gr, r_gr, j, 2, ctx - 3)

    to1, to3 = (ctx + 1 < nctx) & ~last, ctx + 3 < nctx
    hop1, hop3 = first & has1, third & has3
    pass1 = even & has1
    pass3 = odd & has3
    mid_in = ctx >= 2
    bud_in = (even & has1) | (odd & has3)

    def yout_out(j, kind, step):
        to = mate(step)
        part = pl.ds(pl.multiple_of(to * rows, rows), rows)
        return pltpu.make_async_remote_copy(
            src_ref=outb.at[j, pl.ds(2 * kind, 2), :, part],
            dst_ref=out_ref.at[pl.ds(2 * kind, 2), pl.ds(head * held + j * heads, heads)],
            send_sem=s_out.at[j, kind, step - 1],
            recv_sem=r_out.at[j, kind, step - 1],
            device_id=(ctx, to),
            device_id_type=MESH,
        )

    def yout_in(j, kind, step):
        source = lax.rem(head + nhead - step, nhead)
        return pltpu.make_async_remote_copy(
            src_ref=outb.at[j, pl.ds(2 * kind, 2), :, mine],
            dst_ref=out_ref.at[pl.ds(2 * kind, 2), pl.ds(source * held + j * heads, heads)],
            send_sem=s_out.at[j, kind, step - 1],
            recv_sem=r_out.at[j, kind, step - 1],
            device_id=(ctx, source),
            device_id_type=MESH,
        )

    def yout_local(j, kind):
        return pltpu.make_async_copy(
            outb.at[j, pl.ds(2 * kind, 2), :, mine],
            out_ref.at[pl.ds(2 * kind, 2), pl.ds(head * held + j * heads, heads)],
            s_oloc.at[j, kind],
        )

    def yout_start(j, kind):
        for step in range(1, nhead):
            yout_out(j, kind, step).start()
        yout_local(j, kind).start()

    addend = []
    for distance in range(1, R + 1):
        block = ctx - distance
        listed = block == lists_ref[0, 0]
        for entry in range(1, lists_ref.shape[1]):
            listed = listed | (block == lists_ref[0, entry])
        addend.append(jnp.where(listed & (block >= 0), jnp.float32(0), jnp.float32(-jnp.inf)))

    def attend(j, h):
        key0, value0 = blk[j, 0, h], blk[j, 1, h]
        query, grad = blk[j, 2, h], blk[j, 3, h]
        windows = (near, mid, far)
        keys = [key0] + [w[j, 0, h] for w in windows]
        values = [value0] + [w[j, 1, h] for w in windows]
        scores = [dot(k, query, 1, 1) for k in keys]
        s_ids = lax.broadcasted_iota(jnp.int32, (length, length), 0)
        t_ids = lax.broadcasted_iota(jnp.int32, (length, length), 1)
        scores[0] = jnp.where(s_ids <= t_ids, scores[0], -jnp.inf)
        for d in range(1, R + 1):
            scores[d] = scores[d] + addend[d - 1]
        highest = functools.reduce(
            jnp.maximum, [jnp.max(s, axis=0, keepdims=True) for s in scores]
        )
        to_exp2 = score_scale * math.log2(math.e)
        weights = [jnp.exp2((s - highest) * to_exp2) for s in scores]
        total = functools.reduce(
            jnp.add, [jnp.sum(w, axis=0, keepdims=True) for w in weights]
        )
        inverse = 1.0 / total
        probs = [w * inverse for w in weights]
        low = [p.astype(BF16) for p in probs]
        attended = functools.reduce(
            jnp.add, [dot(p, v, 0, 0) for p, v in zip(low, values)]
        ).astype(BF16)
        outb[j, 0, h] = attended
        product = grad.astype(F32) * attended.astype(F32)
        centre = jnp.sum(product.T, axis=0, keepdims=True)
        slopes = [
            (p * (dot(v, grad, 1, 1) - centre)).astype(BF16) for p, v in zip(probs, values)
        ]
        grad_query = functools.reduce(
            jnp.add, [dot(g, k, 0, 0) for g, k in zip(slopes, keys)]
        )
        outb[j, 1, h] = (grad_query * score_scale).astype(BF16)
        for d, slot in enumerate((own, p1, p2, p3)):
            slot[j, 0, h] = (dot(slopes[d], query, 1, 0) * score_scale).astype(slot.dtype)
            slot[j, 1, h] = dot(low[d], grad, 1, 0).astype(slot.dtype)

    order = [(0, 0)]
    for j in range(chunks):
        if j + 1 < chunks:
            order.append((j + 1, 0))
        order.append((j, 1))
    for j, kind in order:
        yin_start(j, kind)
    for distance, slot in ((1, near), (2, mid), (3, far)):

        @pl.when(ctx < distance)
        def _():
            slot[...] = jnp.zeros_like(slot)

    def stage(t, lag, run):
        @pl.when((t >= lag) & (t < lag + chunks))
        def _():
            run(t - lag)

    def forward(j):
        yin_wait(j, 0)
        pl.when(to3)(lambda: send_far(j).start())
        pl.when(to1)(lambda: send_near(j).start())

    def relay(j):
        pl.when(has3)(lambda: send_far(j).wait_recv())
        pl.when(hop3)(lambda: hop_near(j).start())
        pl.when(pass3)(lambda: pass_far(j).start())
        pl.when(has1 & ~first)(lambda: send_near(j).wait_recv())
        pl.when(third)(lambda: pass_near(j).start())

    def relay_again(j):
        @pl.when(hop1)
        def _():
            send_near(j).wait_recv()
            pass_near(j).start()

    def compute(j):
        yin_wait(j, 1)
        pl.when(mid_in)(lambda: pass_near(j).wait_recv())

        def one(h, carry):
            attend(j, h)
            return carry

        lax.fori_loop(0, heads, one, 0)
        pl.when(mid_in)(lambda: give_mid(j).start())
        pl.when(hop1)(lambda: give_far(j).start())
        pl.when(odd)(lambda: give_near(j).start())
        yout_start(j, 0)

    def combine(j):
        pl.when(bud_in)(lambda: give_mid(j).wait_recv())

        @pl.when(pass1)
        def _():
            p1[j] = (p1[j].astype(F32) + bud[j].astype(F32)).astype(BF16)
            pl.when(third)(lambda: give_near(j).start())
            pl.when(first)(lambda: hop_back(j).start())

        @pl.when(pass3)
        def _():
            p3[j] = (p3[j].astype(F32) + bud[j].astype(F32)).astype(BF16)
            give_far(j).start()

    def combine_again(j):
        @pl.when(hop3)
        def _():
            hop_back(j).wait_recv()
            p3[j] = (p3[j].astype(F32) + hop[j].astype(F32)).astype(BF16)
            give_far(j).start()

    def finish(j):
        @pl.when(to1)
        def _():
            give_near(j).wait_recv()
            own[j] = own[j] + ra[j].astype(F32)

        @pl.when(to3)
        def _():
            give_far(j).wait_recv()
            own[j] = own[j] + rb[j].astype(F32)

        outb[j, pl.ds(2, 2)] = own[j].astype(BF16)
        yout_start(j, 1)

    group = 16

    def settle(kind, results):
        def landed(j, carry):
            for step in range(1, nhead):
                yout_in(j, kind, step).wait_recv()
            yout_local(j, kind).wait()
            return carry

        lax.fori_loop(0, chunks, landed, 0)

        def turn(n, carry):
            some = pl.ds(pl.multiple_of(n * group, group), group)
            for a, result in enumerate(results):
                result[some] = jnp.swapaxes(out_ref[2 * kind + a, :, some, :], 0, 1)
            return carry

        lax.fori_loop(0, rows // group, turn, 0)

    def body(t, carry):
        stage(t, 0, forward)
        stage(t, 1, relay)
        stage(t, 3, relay_again)
        stage(t, 5, compute)
        stage(t, 6, combine)
        stage(t, 7, combine_again)
        pl.when(t == chunks + 8)(lambda: settle(0, (out0, out1)))
        stage(t, 9, finish)
        return carry

    lax.fori_loop(0, chunks + 9, body, 0)

    settle(1, (out2, out3))

    def drain(j, carry):
        for kind in range(2):
            for step in range(1, nhead):
                yin_out(j, kind, step).wait_send()
                yout_out(j, kind, step).wait_send()
        pl.when(to1)(lambda: send_near(j).wait_send())
        pl.when(to3)(lambda: send_far(j).wait_send())
        pl.when(pass1)(lambda: pass_near(j).wait_send())
        pl.when(pass3)(lambda: pass_far(j).wait_send())
        pl.when(mid_in)(lambda: give_mid(j).wait_send())
        pl.when(hop3)(lambda: hop_near(j).wait_send())
        pl.when(hop1)(lambda: hop_back(j).wait_send())
        pl.when(has1 & ~first)(lambda: give_near(j).wait_send())
        pl.when(has3)(lambda: give_far(j).wait_send())
        return carry

    lax.fori_loop(0, chunks, drain, 0)


def local(nctx, nhead, queries, keys, values, out_grad, block_lists):
    rows, heads_all, width = queries.shape
    length = rows * nhead
    held = heads_all // nhead
    chunks = 8
    heads = held // chunks
    stacked = jnp.stack([a.transpose(1, 0, 2) for a in (keys, values, queries, out_grad)])
    half = pltpu.VMEM((chunks, 2, heads, length, width), BF16)
    dma = pltpu.SemaphoreType.DMA
    flops = 6 * 2 * held * length * length * (R + 1) * width
    out = pl.pallas_call(
        functools.partial(kernel, nctx, nhead, chunks),
        out_shape=[jax.ShapeDtypeStruct((rows, heads_all, width), BF16)] * 4,
        in_specs=[
            pl.BlockSpec(memory_space=pltpu.SMEM),
            pl.BlockSpec(memory_space=pl.ANY),
        ],
        out_specs=[pl.BlockSpec(memory_space=pltpu.VMEM)] * 4,
        scratch_shapes=[
            pltpu.VMEM((4, heads_all, rows, width), BF16),
            pltpu.VMEM((chunks, 4, heads, length, width), BF16),
            half, half, half,
            half, half, half,
            half, half, half, half,
            pltpu.VMEM((chunks, 2, heads, length, width), F32),
            pltpu.VMEM((chunks, 4, heads, length, width), BF16),
            dma((chunks, 2)),
            dma((chunks, 2, nhead - 1)),
            dma((chunks, 2, nhead - 1)),
            dma((chunks, 4)),
            dma((chunks, 3)),
            dma((chunks, 4)),
            dma((chunks, 4)),
            dma((chunks, 2, nhead - 1)),
            dma((chunks, 2, nhead - 1)),
            dma((chunks, 2)),
        ],
        compiler_params=pltpu.CompilerParams(
            collective_id=0, has_side_effects=True, vmem_limit_bytes=48 * 1024 * 1024
        ),
        cost_estimate=pl.CostEstimate(
            flops=flops, bytes_accessed=16 * rows * heads_all * width, transcendentals=0
        ),
    )(block_lists, stacked)
    return tuple(out)


def solution(mesh):
    split = P(("ctx", "head"), None, None)
    return jax.shard_map(
        functools.partial(local, mesh.shape["ctx"], mesh.shape["head"]),
        mesh=mesh,
        in_specs=(split, split, split, split, P("ctx", None)),
        out_specs=(split, split, split, split),
        check_vma=False,
    )
```

```python
import functools
import math

import jax
import jax.numpy as jnp
from jax import lax
from jax.experimental import pallas as pl
from jax.experimental.pallas import tpu as pltpu
from jax.sharding import PartitionSpec as P

R = 3
MESH = pl.DeviceIdType.MESH
BF16, F32 = jnp.bfloat16, jnp.float32


def dot(a, b, ca, cb):
    return lax.dot_general(a, b, (((ca,), (cb,)), ((), ())), preferred_element_type=F32)


def kernel(
    nctx, nhead, chunks, lists_ref, x_ref, out0, out1, out2, out3,
    out_ref, blk, near, mid, far, p1, p2, p3, bud, hop, ra, rb, own, outb,
    s_loc, s_yin, r_yin, s_ctx, r_ctx, s_gr, r_gr, s_out, r_out, s_oloc,
):
    ctx = lax.axis_index("ctx")
    head = lax.axis_index("head")
    heads = blk.shape[2]
    length = blk.shape[3]
    width = blk.shape[4]
    rows = length // nhead
    held = heads * chunks
    even = lax.rem(ctx, 2) == 0
    odd = lax.rem(ctx, 2) == 1
    place = lax.rem(ctx, 4)
    buddy = ctx + 1 - 2 * lax.rem(ctx, 2)
    score_scale = 1.0 / math.sqrt(width)
    mine = pl.ds(pl.multiple_of(head * rows, rows), rows)

    def mate(step):
        return lax.rem(head + step, nhead)

    barrier = pltpu.get_barrier_semaphore()
    for step in range(1, nhead):
        pl.semaphore_signal(barrier, inc=1, device_id=(ctx, mate(step)), device_id_type=MESH)
    near_by = 0
    for away in (-3, -1, 1, 3):
        other = ctx + away
        inside = (other >= 0) & (other < nctx)

        @pl.when(inside)
        def _():
            pl.semaphore_signal(barrier, inc=1, device_id=(other, head), device_id_type=MESH)

        near_by = near_by + inside.astype(jnp.int32)
    first, third, last = place == 0, place == 2, place == 3
    has1, has3 = ctx >= 1, ctx >= 3
    for role, other in ((third & has3, ctx - 2), (first & has1, ctx + 2)):

        @pl.when(role)
        def _():
            pl.semaphore_signal(barrier, inc=1, device_id=(other, head), device_id_type=MESH)

        near_by = near_by + role.astype(jnp.int32)
    pl.semaphore_wait(barrier, near_by + (nhead - 1))

    def yin_out(j, kind, step):
        to = mate(step)
        return pltpu.make_async_remote_copy(
            src_ref=x_ref.at[pl.ds(2 * kind, 2), pl.ds(to * held + j * heads, heads)],
            dst_ref=blk.at[j, pl.ds(2 * kind, 2), :, mine],
            send_sem=s_yin.at[j, kind, step - 1],
            recv_sem=r_yin.at[j, kind, step - 1],
            device_id=(ctx, to),
            device_id_type=MESH,
        )

    def yin_in(j, kind, step):
        source = lax.rem(head + nhead - step, nhead)
        theirs = pl.ds(pl.multiple_of(source * rows, rows), rows)
        return pltpu.make_async_remote_copy(
            src_ref=x_ref.at[pl.ds(2 * kind, 2), pl.ds(j * heads, heads)],
            dst_ref=blk.at[j, pl.ds(2 * kind, 2), :, theirs],
            send_sem=s_yin.at[j, kind, step - 1],
            recv_sem=r_yin.at[j, kind, step - 1],
            device_id=(ctx, source),
            device_id_type=MESH,
        )

    def yin_local(j, kind):
        return pltpu.make_async_copy(
            x_ref.at[pl.ds(2 * kind, 2), pl.ds(head * held + j * heads, heads)],
            blk.at[j, pl.ds(2 * kind, 2), :, mine],
            s_loc.at[j, kind],
        )

    def yin_start(j, kind):
        for step in range(1, nhead):
            yin_out(j, kind, step).start()
        yin_local(j, kind).start()

    def yin_wait(j, kind):
        for step in range(1, nhead):
            yin_in(j, kind, step).wait_recv()
        yin_local(j, kind).wait()

    def ctx_copy(src, dst, sems, recvs, j, which, to, lands=None):
        return pltpu.make_async_remote_copy(
            src_ref=src,
            dst_ref=dst,
            send_sem=sems.at[j, which],
            recv_sem=recvs.at[j, which if lands is None else lands],
            device_id=(to, head),
            device_id_type=MESH,
        )

    def kv(j):
        return blk.at[j, pl.ds(0, 2)]

    def send_near(j):
        return ctx_copy(kv(j), near.at[j], s_ctx, r_ctx, j, 0, ctx + 1)

    def send_far(j):
        return ctx_copy(kv(j), far.at[j], s_ctx, r_ctx, j, 1, ctx + 3)

    def pass_near(j):
        return ctx_copy(near.at[j], mid.at[j], s_ctx, r_ctx, j, 2, buddy)

    def pass_far(j):
        return ctx_copy(far.at[j], mid.at[j], s_ctx, r_ctx, j, 2, buddy)

    def hop_near(j):
        return ctx_copy(far.at[j], near.at[j], s_ctx, r_ctx, j, 3, ctx - 2, 0)

    def hop_back(j):
        return ctx_copy(p1.at[j], hop.at[j], s_gr, r_gr, j, 3, ctx + 2)

    def give_mid(j):
        return ctx_copy(p2.at[j], bud.at[j], s_gr, r_gr, j, 0, buddy)

    def give_near(j):
        return ctx_copy(p1.at[j], ra.at[j], s_gr, r_gr, j, 1, ctx - 1)

    def give_far(j):
        return ctx_copy(p3.at[j], rb.at[j], s_gr, r_gr, j, 2, ctx - 3)

    to1, to3 = (ctx + 1 < nctx) & ~last, ctx + 3 < nctx
    hop1, hop3 = first & has1, third & has3
    pass1 = even & has1
    pass3 = odd & has3
    mid_in = ctx >= 2
    bud_in = (even & has1) | (odd & has3)

    def yout_out(j, kind, step):
        to = mate(step)
        part = pl.ds(pl.multiple_of(to * rows, rows), rows)
        return pltpu.make_async_remote_copy(
            src_ref=outb.at[j, pl.ds(2 * kind, 2), :, part],
            dst_ref=out_ref.at[pl.ds(2 * kind, 2), pl.ds(head * held + j * heads, heads)],
            send_sem=s_out.at[j, kind, step - 1],
            recv_sem=r_out.at[j, kind, step - 1],
            device_id=(ctx, to),
            device_id_type=MESH,
        )

    def yout_in(j, kind, step):
        source = lax.rem(head + nhead - step, nhead)
        return pltpu.make_async_remote_copy(
            src_ref=outb.at[j, pl.ds(2 * kind, 2), :, mine],
            dst_ref=out_ref.at[pl.ds(2 * kind, 2), pl.ds(source * held + j * heads, heads)],
            send_sem=s_out.at[j, kind, step - 1],
            recv_sem=r_out.at[j, kind, step - 1],
            device_id=(ctx, source),
            device_id_type=MESH,
        )

    def yout_local(j, kind):
        return pltpu.make_async_copy(
            outb.at[j, pl.ds(2 * kind, 2), :, mine],
            out_ref.at[pl.ds(2 * kind, 2), pl.ds(head * held + j * heads, heads)],
            s_oloc.at[j, kind],
        )

    def yout_start(j, kind):
        for step in range(1, nhead):
            yout_out(j, kind, step).start()
        yout_local(j, kind).start()

    addend = []
    for distance in range(1, R + 1):
        block = ctx - distance
        listed = block == lists_ref[0, 0]
        for entry in range(1, lists_ref.shape[1]):
            listed = listed | (block == lists_ref[0, entry])
        addend.append(jnp.where(listed & (block >= 0), jnp.float32(0), jnp.float32(-jnp.inf)))

    def attend(j, h):
        key0, value0 = blk[j, 0, h], blk[j, 1, h]
        query, grad = blk[j, 2, h], blk[j, 3, h]
        windows = (near, mid, far)
        keys = [key0] + [w[j, 0, h] for w in windows]
        values = [value0] + [w[j, 1, h] for w in windows]
        scores = [dot(k, query, 1, 1) for k in keys]
        s_ids = lax.broadcasted_iota(jnp.int32, (length, length), 0)
        t_ids = lax.broadcasted_iota(jnp.int32, (length, length), 1)
        scores[0] = jnp.where(s_ids <= t_ids, scores[0], -jnp.inf)
        for d in range(1, R + 1):
            scores[d] = scores[d] + addend[d - 1]
        highest = functools.reduce(
            jnp.maximum, [jnp.max(s, axis=0, keepdims=True) for s in scores]
        )
        to_exp2 = score_scale * math.log2(math.e)
        weights = [jnp.exp2((s - highest) * to_exp2) for s in scores]
        total = functools.reduce(
            jnp.add, [jnp.sum(w, axis=0, keepdims=True) for w in weights]
        )
        inverse = 1.0 / total
        probs = [w * inverse for w in weights]
        low = [p.astype(BF16) for p in probs]
        attended = functools.reduce(
            jnp.add, [dot(p, v, 0, 0) for p, v in zip(low, values)]
        ).astype(BF16)
        outb[j, 0, h] = attended
        product = grad.astype(F32) * attended.astype(F32)
        centre = jnp.sum(product.T, axis=0, keepdims=True)
        slopes = [
            (p * (dot(v, grad, 1, 1) - centre)).astype(BF16) for p, v in zip(probs, values)
        ]
        grad_query = functools.reduce(
            jnp.add, [dot(g, k, 0, 0) for g, k in zip(slopes, keys)]
        )
        outb[j, 1, h] = (grad_query * score_scale).astype(BF16)
        for d, slot in enumerate((own, p1, p2, p3)):
            slot[j, 0, h] = (dot(slopes[d], query, 1, 0) * score_scale).astype(slot.dtype)
            slot[j, 1, h] = dot(low[d], grad, 1, 0).astype(slot.dtype)

    order = [(0, 0)]
    for j in range(chunks):
        if j + 1 < chunks:
            order.append((j + 1, 0))
        order.append((j, 1))
    for j, kind in order:
        yin_start(j, kind)
    for distance, slot in ((1, near), (2, mid), (3, far)):

        @pl.when(ctx < distance)
        def _():
            slot[...] = jnp.zeros_like(slot)

    def stage(t, lag, run):
        @pl.when((t >= lag) & (t < lag + chunks))
        def _():
            run(t - lag)

    def forward(j):
        yin_wait(j, 0)
        pl.when(to3)(lambda: send_far(j).start())
        pl.when(to1)(lambda: send_near(j).start())

    def relay(j):
        pl.when(has3)(lambda: send_far(j).wait_recv())
        pl.when(hop3)(lambda: hop_near(j).start())
        pl.when(pass3)(lambda: pass_far(j).start())
        pl.when(has1 & ~first)(lambda: send_near(j).wait_recv())
        pl.when(third)(lambda: pass_near(j).start())

    def relay_again(j):
        @pl.when(hop1)
        def _():
            send_near(j).wait_recv()
            pass_near(j).start()

    def compute(j):
        yin_wait(j, 1)
        pl.when(mid_in)(lambda: pass_near(j).wait_recv())

        def one(h, carry):
            attend(j, h)
            return carry

        lax.fori_loop(0, heads, one, 0)
        pl.when(mid_in)(lambda: give_mid(j).start())
        pl.when(hop1)(lambda: give_far(j).start())
        pl.when(odd)(lambda: give_near(j).start())
        yout_start(j, 0)

    def combine(j):
        pl.when(bud_in)(lambda: give_mid(j).wait_recv())

        @pl.when(pass1)
        def _():
            p1[j] = (p1[j].astype(F32) + bud[j].astype(F32)).astype(BF16)
            pl.when(third)(lambda: give_near(j).start())
            pl.when(first)(lambda: hop_back(j).start())

        @pl.when(pass3)
        def _():
            p3[j] = (p3[j].astype(F32) + bud[j].astype(F32)).astype(BF16)
            give_far(j).start()

    def combine_again(j):
        @pl.when(hop3)
        def _():
            hop_back(j).wait_recv()
            p3[j] = (p3[j].astype(F32) + hop[j].astype(F32)).astype(BF16)
            give_far(j).start()

    def finish(j):
        @pl.when(to1)
        def _():
            give_near(j).wait_recv()
            own[j] = own[j] + ra[j].astype(F32)

        @pl.when(to3)
        def _():
            give_far(j).wait_recv()
            own[j] = own[j] + rb[j].astype(F32)

        outb[j, pl.ds(2, 2)] = own[j].astype(BF16)
        yout_start(j, 1)

    group = 16

    def settle(kind, results):
        def landed(j, carry):
            for step in range(1, nhead):
                yout_in(j, kind, step).wait_recv()
            yout_local(j, kind).wait()
            return carry

        lax.fori_loop(0, chunks, landed, 0)

        def turn(n, carry):
            some = pl.ds(pl.multiple_of(n * group, group), group)
            for a, result in enumerate(results):
                result[some] = jnp.swapaxes(out_ref[2 * kind + a, :, some, :], 0, 1)
            return carry

        lax.fori_loop(0, rows // group, turn, 0)

    def body(t, carry):
        stage(t, 3, relay_again)
        stage(t, 1, relay)
        stage(t, 0, forward)
        stage(t, 5, compute)
        stage(t, 6, combine)
        stage(t, 7, combine_again)
        pl.when(t == chunks + 8)(lambda: settle(0, (out0, out1)))
        stage(t, 9, finish)
        return carry

    lax.fori_loop(0, chunks + 9, body, 0)

    settle(1, (out2, out3))

    def drain(j, carry):
        for kind in range(2):
            for step in range(1, nhead):
                yin_out(j, kind, step).wait_send()
                yout_out(j, kind, step).wait_send()
        pl.when(to1)(lambda: send_near(j).wait_send())
        pl.when(to3)(lambda: send_far(j).wait_send())
        pl.when(pass1)(lambda: pass_near(j).wait_send())
        pl.when(pass3)(lambda: pass_far(j).wait_send())
        pl.when(mid_in)(lambda: give_mid(j).wait_send())
        pl.when(hop3)(lambda: hop_near(j).wait_send())
        pl.when(hop1)(lambda: hop_back(j).wait_send())
        pl.when(has1 & ~first)(lambda: give_near(j).wait_send())
        pl.when(has3)(lambda: give_far(j).wait_send())
        return carry

    lax.fori_loop(0, chunks, drain, 0)


def local(nctx, nhead, queries, keys, values, out_grad, block_lists):
    rows, heads_all, width = queries.shape
    length = rows * nhead
    held = heads_all // nhead
    chunks = 8
    heads = held // chunks
    stacked = jnp.stack([a.transpose(1, 0, 2) for a in (keys, values, queries, out_grad)])
    half = pltpu.VMEM((chunks, 2, heads, length, width), BF16)
    dma = pltpu.SemaphoreType.DMA
    flops = 6 * 2 * held * length * length * (R + 1) * width
    out = pl.pallas_call(
        functools.partial(kernel, nctx, nhead, chunks),
        out_shape=[jax.ShapeDtypeStruct((rows, heads_all, width), BF16)] * 4,
        in_specs=[
            pl.BlockSpec(memory_space=pltpu.SMEM),
            pl.BlockSpec(memory_space=pl.ANY),
        ],
        out_specs=[pl.BlockSpec(memory_space=pltpu.VMEM)] * 4,
        scratch_shapes=[
            pltpu.VMEM((4, heads_all, rows, width), BF16),
            pltpu.VMEM((chunks, 4, heads, length, width), BF16),
            half, half, half,
            half, half, half,
            half, half, half, half,
            pltpu.VMEM((chunks, 2, heads, length, width), F32),
            pltpu.VMEM((chunks, 4, heads, length, width), BF16),
            dma((chunks, 2)),
            dma((chunks, 2, nhead - 1)),
            dma((chunks, 2, nhead - 1)),
            dma((chunks, 4)),
            dma((chunks, 3)),
            dma((chunks, 4)),
            dma((chunks, 4)),
            dma((chunks, 2, nhead - 1)),
            dma((chunks, 2, nhead - 1)),
            dma((chunks, 2)),
        ],
        compiler_params=pltpu.CompilerParams(
            collective_id=0, has_side_effects=True, vmem_limit_bytes=48 * 1024 * 1024
        ),
        cost_estimate=pl.CostEstimate(
            flops=flops, bytes_accessed=16 * rows * heads_all * width, transcendentals=0
        ),
    )(block_lists, stacked)
    return tuple(out)


def solution(mesh):
    split = P(("ctx", "head"), None, None)
    return jax.shard_map(
        functools.partial(local, mesh.shape["ctx"], mesh.shape["head"]),
        mesh=mesh,
        in_specs=(split, split, split, split, P("ctx", None)),
        out_specs=(split, split, split, split),
        check_vma=False,
    )
```
